32 devices in a mesh: dp: 8 (over y, x, core), tp: 4 (over z).
Axes of the slice: x: 2, y: 2, z: 4, core: 2. Of those that a mesh axis runs over, the one named last changes fastest.
Arguments:
- hidden_states: bfloat16 [4096, 3, 4096], P('dp', None, 'tp'), may hold values from -6 to 6
- fc_weight: bfloat16 [4096, 3, 4096], P('dp', None, 'tp'), may hold values from -0.0546875 to 0.0546875
- norm_gain: float32 [4096], replicated, may hold values from 0.1 to 1.9
- upstream: bfloat16 [4096, 4096], P(('dp', 'tp')), may hold values from -0.1875 to 0.1875
- lengths: int32 [32], P(('dp', 'tp')), may hold values from 1 to 128, as said below
Outputs:
- normed: bfloat16 [4096, 4096], P(('dp', 'tp'))
- grad_weight: float32 [4096, 3, 4096], P('dp', None, 'tp')
- grad_gain: float32 [4096], replicated
The draws below stay inside these ranges and needn't reach their ends.
Inputs may be any that keep to these rules, and one draw needn't show every extreme that they name: `lengths`: some sample carries loss at all 128 positions.
All inputs are finite; a program needn't handle non-finite values.
Results may differ from the reference program's by a relative error of at most 0.014.
Values may be sent and summed in bfloat16 or wider, within the bound.
A program may use at most 128 MiB of HBM per device.

```python
import jax
import jax.numpy as jnp
from jax import lax

HIDDEN_SIZE = 4096
DRAFT = 4096
LAYERS = 3
TOK_DEV = 128
TOKENS = 4096
SAMPLES = 32
N_DP = 8
N_TP = 4


def draw_lengths(key, part):
    first_key = jax.random.fold_in(key, 11)
    second_key = jax.random.fold_in(key, 23)
    values = jax.random.randint(first_key, (SAMPLES,), 1, TOK_DEV + 1, dtype=jnp.int32)
    chosen = jax.random.randint(second_key, (), 0, SAMPLES, dtype=jnp.int32)
    return values.at[chosen].set(TOK_DEV)


def with_spikes(values, stream_key, source, target, parts, factor):
    owner, partner = [(jnp.arange(values.shape[position]) // (values.shape[position] // parts)).reshape([-1 if axis == position else 1 for axis in range(values.ndim)]) for position in (source, target)]
    chosen = jax.random.permutation(stream_key, parts)[partner]
    strong = (owner == chosen) | (owner == (partner + parts // 2) % parts)
    return jnp.where(strong, factor * values, values)


def block_levels(key, extent, cuts, least, top_value):
    gain, own = 1.0, jax.random.fold_in(key, 6)
    for position, blocks in cuts:
        steps = jnp.exp(jax.random.uniform(jax.random.fold_in(own, position), (blocks,), jnp.float32, least / len(cuts), top_value / len(cuts)))
        gain = gain * jnp.repeat(steps, extent[position] // blocks).reshape([-1 if axis == position else 1 for axis in range(len(extent))])
    return gain


def scatter_about(key, dims, spread, most, shards=(), kind=jnp.bfloat16):
    entries = spread * jax.random.normal(key, dims, jnp.float32)
    if shards:
        entries = entries * block_levels(key, dims, shards, -0.22, 0.18)
    return jnp.clip(entries, -most, most).astype(kind)


def heavy_noise(rng, shape, scale, bound, split, heavy, held_as=jnp.bfloat16):
    result = scale * jax.random.normal(rng, shape, jnp.float32)
    if split:
        result = result * block_levels(rng, shape, split, -0.22, 0.18)
    return jnp.clip(with_spikes(result, jax.random.fold_in(rng, 3), *heavy), -bound, bound).astype(held_as)


def setup_inputs(seed: int = 0) -> dict:
    key_of = jax.random.split(jax.random.key(seed), 6)
    hidden_states = scatter_about(key_of[0], (TOKENS, LAYERS, HIDDEN_SIZE), 1.0, 6.0, ((0, 8), (2, 4)))
    fc_weight = scatter_about(key_of[1], (DRAFT, LAYERS, HIDDEN_SIZE), (LAYERS * HIDDEN_SIZE) ** -0.5, 0.0546875, ((0, 8), (2, 4)))
    norm_gain = jnp.clip(1.0 + 0.18 * jax.random.normal(key_of[2], (DRAFT,), jnp.float32), 0.1, 1.9)
    upstream = heavy_noise(key_of[3], (TOKENS, DRAFT), TOKENS ** -0.5, 0.1875, ((0, 32),), (0, 1, 32, 2.75))
    lengths = draw_lengths(jax.random.fold_in(key_of[5], 71), 0)
    return {"hidden_states": hidden_states, "fc_weight": fc_weight, "norm_gain": norm_gain, "upstream": upstream, "lengths": lengths}


def round_trip(values):
    return lax.optimization_barrier(values.astype(jnp.bfloat16)).astype(jnp.float32)

def reference(hidden_states, fc_weight, norm_gain, upstream, lengths):
    tokens = hidden_states.shape[0]
    slab_width = HIDDEN_SIZE // N_TP
    merged = jnp.zeros((tokens, DRAFT), jnp.float32)
    for tp_index in range(N_TP):
        offset = tp_index * slab_width
        hidden_part = hidden_states[:, :, offset:offset + slab_width].reshape(tokens, LAYERS * slab_width)
        weight_part = fc_weight[:, :, offset:offset + slab_width].reshape(DRAFT, LAYERS * slab_width)
        product = lax.dot_general(hidden_part, weight_part, (((1,), (1,)), ((), ())), preferred_element_type=jnp.float32)
        merged = merged + round_trip(product)
    squares = lax.optimization_barrier(jnp.mean(merged * merged, axis=1, keepdims=True))
    inverse = lax.rsqrt(squares + 1e-05)
    scaled = merged * inverse
    normed = (scaled * norm_gain).astype(jnp.bfloat16)
    positions = jnp.arange(tokens, dtype=jnp.int32)
    owners = (positions // TOK_DEV).astype(jnp.int32)
    live_mask = (positions % TOK_DEV < lengths[owners]).astype(jnp.float32)
    incoming = upstream.astype(jnp.float32) * live_mask[:, None]
    grad_gain = lax.optimization_barrier(jnp.sum(incoming * scaled, axis=0))
    grad_scaled = incoming * norm_gain
    projection = lax.optimization_barrier(jnp.mean(grad_scaled * scaled, axis=1, keepdims=True))
    grad_merged = (inverse * (grad_scaled - scaled * projection)).astype(jnp.bfloat16)
    group_size = tokens // N_DP
    grad_weight = jnp.zeros((DRAFT, LAYERS * HIDDEN_SIZE), jnp.float32)
    for dp_index in range(N_DP):
        offset = dp_index * group_size
        grad_part = grad_merged[offset:offset + group_size]
        hidden_part = hidden_states[offset:offset + group_size].reshape(group_size, LAYERS * HIDDEN_SIZE)
        product = lax.dot_general(grad_part, hidden_part, (((0,), (0,)), ((), ())), preferred_element_type=jnp.float32)
        grad_weight = grad_weight + round_trip(product)
    return (normed, grad_weight.reshape(DRAFT, LAYERS, HIDDEN_SIZE), grad_gain)
```

```python
import jax
import jax.numpy as jnp
from jax import lax
from jax.sharding import PartitionSpec as P


def body(hidden_states, fc_weight, norm_gain, upstream, lengths):
    tok_group, layers, slab = hidden_states.shape
    rows = fc_weight.shape[0]
    tok_dev, draft = upstream.shape
    dp, tp = lax.axis_size("dp"), lax.axis_size("tp")
    inner = 4 if dp % 4 == 0 else 1
    outer = dp // inner
    near = [[o * inner + i for i in range(inner)] for o in range(outer)]
    far = [[o * inner + i for o in range(outer)] for i in range(inner)]
    depth = layers * slab
    width = outer * rows

    hidden = lax.all_gather(hidden_states, "dp", axis=0, tiled=True, axis_index_groups=near)
    weight = lax.all_gather(fc_weight, "dp", axis=0, tiled=True, axis_index_groups=far)
    lens = lax.all_gather(lengths, "dp", axis=0, tiled=True, axis_index_groups=near)
    up = upstream.reshape(tok_dev, outer, inner, rows).transpose(2, 0, 1, 3).reshape(inner, tok_dev, width)
    up = lax.all_to_all(up, "dp", 0, 0, axis_index_groups=near)
    mine = lax.axis_index("dp") % inner
    gain = lax.dynamic_index_in_dim(norm_gain.reshape(outer, inner, rows), mine, 1, keepdims=False).reshape(width)

    flat_h = hidden.reshape(inner, tp, tok_dev, depth).transpose(1, 0, 2, 3).reshape(tp * inner * tok_dev, depth)
    flat_w = weight.reshape(width, depth)
    sums = lax.dot_general(flat_h, flat_w, (((1,), (1,)), ((), ())), preferred_element_type=jnp.float32)
    merged = lax.psum_scatter(sums.astype(jnp.bfloat16), "tp", scatter_dimension=0, tiled=True).astype(jnp.float32)
    merged = merged.reshape(inner, tok_dev, width)
    pos = lax.broadcasted_iota(jnp.int32, (inner, tok_dev, 1), 1)
    live = (pos < lens[:, None, None]).astype(jnp.float32)
    incoming = up.astype(jnp.float32) * live
    along = incoming * gain
    stats = jnp.stack([jnp.sum(merged * merged, axis=2), jnp.sum(along * merged, axis=2)])
    stats = lax.psum(stats, "dp", axis_index_groups=near) / draft
    inverse = lax.rsqrt(stats[0] + 1e-05)[:, :, None]
    scaled = merged * inverse
    proj = stats[1][:, :, None] * inverse
    normed = (scaled * gain).astype(jnp.bfloat16)
    normed = lax.all_to_all(normed, "dp", 0, 0, axis_index_groups=near)
    normed = normed.reshape(inner, tok_dev, outer, rows).transpose(1, 2, 0, 3).reshape(tok_dev, draft)
    ggain = jnp.sum(incoming * scaled, axis=(0, 1))
    full = jnp.zeros((outer, inner, rows), jnp.float32)
    full = lax.dynamic_update_slice(full, ggain.reshape(outer, 1, rows), (0, mine, 0)).reshape(draft)
    grad_gain = lax.psum(full, ("dp", "tp"))
    grad_m = (inverse * (along - scaled * proj)).astype(jnp.bfloat16).reshape(inner * tok_dev, width)
    grad_all = lax.all_gather(grad_m, "tp", axis=0, tiled=True)
    product = lax.dot_general(grad_all, flat_h, (((0,), (0,)), ((), ())), preferred_element_type=jnp.float32)
    grad_weight = lax.psum_scatter(
        product.reshape(width, layers, slab).astype(jnp.bfloat16), "dp",
        scatter_dimension=0, tiled=True, axis_index_groups=far).astype(jnp.float32)
    return normed, grad_weight, grad_gain


def solution(mesh):
    return jax.shard_map(
        body,
        mesh=mesh,
        in_specs=(
            P("dp", None, "tp"),
            P("dp", None, "tp"),
            P(),
            P(("dp", "tp"), None),
            P(("dp", "tp")),
        ),
        out_specs=(P(("dp", "tp"), None), P("dp", None, "tp"), P()),
        check_vma=False,
    )
```

```python
import functools

import jax
import jax.numpy as jnp
from jax import lax
from jax.experimental import pallas as pl
from jax.experimental.pallas import tpu as pltpu
from jax.sharding import PartitionSpec as P

MESH = pl.DeviceIdType.MESH
INNER = 4


def kernel(dp, tp, pieces, h_ref, w_ref, up_ref, gain_ref, normed_ref, gw_ref, gg_ref,
           h_all, w_all, stage, parts, merged, up_all, norm_buf, gmt, gstage, grecv,
           st, st_all, gg, gg_tp, gg_out, gg_in,
           local_sem, hs, hr, ws, wr, us, ur, rs_s, rs_r, st_s, st_r, ag_s, ag_r,
           ns, nr, gs, gr, g1s, g1r, g2s, g2r, g3s, g3r):
    outer = dp // INNER
    d, t = lax.axis_index("dp"), lax.axis_index("tp")
    o, i = d // INNER, d % INNER
    x, c = i // 2, i % 2
    tok = h_ref.shape[1]
    depth = h_ref.shape[2]
    chunks, chunk = w_all.shape[0], w_all.shape[1]
    per = chunks // outer
    rows = per * chunk
    draft = dp * rows
    half = tp // 2

    def inner_of(s):
        return ((x + s // 2) % 2) * 2 + (c + s % 2) % 2

    def near(s):
        return {"dp": o * INNER + inner_of(s)}

    def far(r):
        return {"dp": ((o + r) % outer) * INNER + i}

    def columns(block_o, block_i):
        return pl.ds(pl.multiple_of((block_o * INNER + block_i) * rows, 128), rows)

    def rdma(src, dst, ssem, rsem, dev):
        return pltpu.make_async_remote_copy(src_ref=src, dst_ref=dst, send_sem=ssem, recv_sem=rsem,
                                            device_id=dev, device_id_type=MESH)

    started = []

    def send(src, dst, ssem, rsem, dev):
        copy = rdma(src, dst, ssem, rsem, dev)
        copy.start()
        started.append(copy)

    mine = [pltpu.make_async_copy(h_ref, h_all.at[:, 0], local_sem.at[0]),
            pltpu.make_async_copy(w_ref, w_all.at[pl.ds(0, per)], local_sem.at[1])]
    for r in range(outer):
        mine.append(pltpu.make_async_copy(up_ref.at[:, columns((o + r) % outer, i)], up_all.at[0, r],
                                          local_sem.at[2 + r]))
    for copy in mine:
        copy.start()

    barrier = pltpu.get_barrier_semaphore()
    partners = ([near(s) for s in range(1, INNER)] + [far(r) for r in range(1, outer)]
                + [{"tp": (t + q) % tp} for q in range(1, tp)])
    for dev in partners:
        pl.semaphore_signal(barrier, inc=1, device_id=dev, device_id_type=MESH)
    pl.semaphore_wait(barrier, len(partners))

    def zpart(p):
        return pl.ds(p * (tp // pieces), tp // pieces)

    for p in range(pieces):
        send(h_ref.at[zpart(p)], h_all.at[zpart(p), 2], hs.at[0, p], hr.at[2, p], near(2))
    for r in range(1, outer):
        for j in range(per):
            slot = (outer - r) * per + j
            send(w_ref.at[j], w_all.at[slot], ws.at[slot], wr.at[slot], far(r))
    for p in range(pieces):
        send(h_ref.at[zpart(p)], h_all.at[zpart(p), 1], hs.at[1, p], hr.at[1, p], near(1))
    for s in range(1, INNER):
        for r in range(outer):
            send(up_ref.at[:, columns((o + r) % outer, inner_of(s))], up_all.at[s, r],
                 us.at[s, r], ur.at[s, r], near(s))

    def rs_copy(z, wc, s, src):
        return rdma(stage.at[wc, z, s], parts.at[src, wc, s], rs_s.at[z, wc, s],
                    rs_r.at[src, wc, s], {"tp": z})

    def product(z0, nz, s, wc):
        left = h_all[z0:z0 + nz, s].reshape(nz * tok, depth)
        out = lax.dot_general(left, w_all[wc], (((1,), (1,)), ((), ())),
                              preferred_element_type=jnp.float32)
        stage[wc, z0:z0 + nz, s] = out.astype(jnp.bfloat16).reshape(nz, tok, chunk)
        for z in range(z0, z0 + nz):
            @pl.when(t != z)
            def _():
                rs_copy(z, wc, s, t).start()

    def over(lo, hi, fn):
        def step(k, carry):
            fn(k)
            return carry
        lax.fori_loop(lo, hi, step, 0)

    mine[0].wait()
    mine[1].wait()
    over(0, per, lambda wc: product(0, tp, 0, wc))
    for p in range(pieces):
        rdma(h_ref.at[zpart(p)], h_all.at[zpart(p), 1], hs.at[1, p], hr.at[1, p], near(1)).wait_recv()
    over(0, per, lambda wc: product(0, tp, 1, wc))

    have_w, have_h = per, 0
    step_z = tp // pieces
    while have_w < chunks or have_h < pieces:
        if have_h < pieces:
            p = have_h
            rdma(h_ref.at[zpart(p)], h_all.at[zpart(p), 2], hs.at[0, p], hr.at[2, p], near(2)).wait_recv()
            send(h_all.at[zpart(p), 2], h_all.at[zpart(p), 3], hs.at[2, p], hr.at[3, p], near(1))
        if have_w < chunks:
            wc = have_w
            rdma(w_ref.at[0], w_all.at[wc], ws.at[wc], wr.at[wc], far(1)).wait_recv()
            over(0, 2, lambda s: product(0, tp, s, wc))
            for p in range(have_h):
                over(2, INNER, lambda s: product(p * step_z, step_z, s, wc))
            have_w += 1
        if have_h < pieces:
            p = have_h
            over(0, have_w, lambda wc: product(p * step_z, step_z, 2, wc))
            rdma(h_all.at[zpart(p), 2], h_all.at[zpart(p), 3], hs.at[2, p], hr.at[3, p], near(1)).wait_recv()
            over(0, have_w, lambda wc: product(p * step_z, step_z, 3, wc))
            have_h += 1

    for copy in mine[2:]:
        copy.wait()
    for s in range(1, INNER):
        for r in range(outer):
            rdma(up_ref.at[:, columns(o, i)], up_all.at[s, r], us.at[s, r], ur.at[s, r], near(s)).wait_recv()

    def gain_of(wc):
        r, j = wc // per, wc % per
        return gain_ref[(o + r) % outer, i, j]

    for s in range(INNER):
        sq = jnp.zeros((tok, 1), jnp.float32)
        al = jnp.zeros((tok, 1), jnp.float32)
        for wc in range(chunks):
            r, j = wc // per, wc % per
            total = stage[wc, t, s].astype(jnp.float32)
            for q in range(1, tp):
                src = (t + q) % tp
                rs_copy(t, wc, s, src).wait_recv()
                total = total + parts[src, wc, s].astype(jnp.float32)
            merged[s, wc] = total
            along = up_all[s, r, :, j * chunk:(j + 1) * chunk].astype(jnp.float32) * gain_of(wc)
            sq = sq + jnp.sum(total * total, axis=1, keepdims=True)
            al = al + jnp.sum(total * along, axis=1, keepdims=True)
        st[s:s + 1, :] = jnp.swapaxes(jnp.broadcast_to(sq, (tok, 128)), 0, 1)[0:1, :]
        st[INNER + s:INNER + s + 1, :] = jnp.swapaxes(jnp.broadcast_to(al, (tok, 128)), 0, 1)[0:1, :]
    for s in range(1, INNER):
        send(st, st_all.at[s], st_s.at[s], st_r.at[s], near(s))
    for s in range(1, INNER):
        rdma(st, st_all.at[s], st_s.at[s], st_r.at[s], near(s)).wait_recv()

    inverse, proj = [], []
    for s in range(INNER):
        sq, al = st[s:s + 1, :], st[INNER + s:INNER + s + 1, :]
        for q in range(1, INNER):
            k = ((s // 2 + q // 2) % 2) * 2 + (s + q) % 2
            sq = sq + st_all[q, k:k + 1, :]
            al = al + st_all[q, INNER + k:INNER + k + 1, :]
        inv = lax.rsqrt(sq / draft + 1e-05)
        pr = al * inv / draft
        inverse.append(jnp.swapaxes(jnp.broadcast_to(inv, (128, tok)), 0, 1)[:, 0:1])
        proj.append(jnp.swapaxes(jnp.broadcast_to(pr, (128, tok)), 0, 1)[:, 0:1])

    def ag_copy(wc, q, src):
        return rdma(gmt.at[wc, src], gmt.at[wc, src], ag_s.at[wc, q], ag_r.at[wc, src],
                    {"tp": (t + q) % tp})

    order = list(range(per, chunks)) + list(range(per))
    for wc in order:
        r, j = wc // per, wc % per
        gain = gain_of(wc)
        own = jnp.zeros((1, chunk), jnp.float32)
        for s in range(INNER):
            scaled = merged[s, wc] * inverse[s]
            incoming = up_all[s, r, :, j * chunk:(j + 1) * chunk].astype(jnp.float32)
            norm_buf[s, r, :, j * chunk:(j + 1) * chunk] = (scaled * gain).astype(jnp.bfloat16)
            own = own + jnp.sum(incoming * scaled, axis=0, keepdims=True)
            grad = inverse[s] * (incoming * gain - scaled * proj[s])
            gmt[wc, t, :, s * tok:(s + 1) * tok] = jnp.swapaxes(grad, 0, 1).astype(jnp.bfloat16)
        gg[wc:wc + 1, :] = own
        for q in range(1, tp):
            ag_copy(wc, q, t).start()

    for s in range(1, INNER):
        for r in range(outer):
            send(norm_buf.at[s, r], normed_ref.at[:, columns((o + r) % outer, i)],
                 ns.at[s, r], nr.at[s, r], near(s))
    keep = []
    for r in range(outer):
        copy = pltpu.make_async_copy(norm_buf.at[0, r], normed_ref.at[:, columns((o + r) % outer, i)],
                                     local_sem.at[2 + r])
        copy.start()
        keep.append(copy)
    for q in range(1, tp):
        send(gg, gg_tp.at[tp - q], g1s.at[q], g1r.at[tp - q], {"tp": (t + q) % tp})

    def gain_step(n):
        if n == 0:
            total = gg[...]
            for q in range(1, tp):
                rdma(gg, gg_tp.at[q], g1s.at[q], g1r.at[q], {"tp": (t + q) % tp}).wait_recv()
                total = total + gg_tp[q]
            gg_out[0] = total
            for r in range(1, outer):
                send(gg_out.at[0], gg_out.at[outer - r], g2s.at[r], g2r.at[outer - r], far(r))
        if n == 1:
            for r in range(1, outer):
                rdma(gg_out.at[0], gg_out.at[r], g2s.at[r], g2r.at[r], far(r)).wait_recv()
            for wc in range(chunks):
                total = gg_out[0, wc:wc + 1, :]
                for r in range(1, outer):
                    k = (wc - r * per) % chunks
                    total = total + gg_out[r, k:k + 1, :]
                gg_in[0, wc:wc + 1, :] = total
            for s in range(1, INNER):
                send(gg_in.at[0], gg_in.at[s], g3s.at[s], g3r.at[s], near(s))
        if n == 2:
            for s in range(1, INNER):
                rdma(gg_in.at[0], gg_in.at[s], g3s.at[s], g3r.at[s], near(s)).wait_recv()
            for s in range(INNER):
                for wc in range(chunks):
                    gg_ref[(o + wc // per) % outer, inner_of(s), wc % per] = gg_in[s, wc:wc + 1, :]

    tile = 512
    for n, wc in enumerate(order):
        for q in range(1, tp):
            ag_copy(wc, q, (t + q) % tp).wait_recv()

        def step(k, carry):
            cols = pl.ds(pl.multiple_of(k * tile, 128), tile)
            acc = jnp.zeros((chunk, tile), jnp.float32)
            for z in range(tp):
                right = h_all[z, :, :, cols].reshape(INNER * tok, tile)
                acc = acc + jnp.dot(gmt[wc, z], right, preferred_element_type=jnp.float32)
            if wc >= per:
                gstage[wc - per, :, cols] = acc.astype(jnp.bfloat16)
            else:
                gw_ref[wc, :, cols] = acc
            return carry
        lax.fori_loop(0, depth // tile, step, 0)
        if wc >= per:
            r, j = wc // per, wc % per
            slot = (outer - r - 1) * per + j
            send(gstage.at[wc - per], grecv.at[slot], gs.at[slot], gr.at[slot], far(r))
        gain_step(n)
    for j in range(per):
        for r in range(1, outer):
            slot = (r - 1) * per + j
            rdma(gstage.at[0], grecv.at[slot], gs.at[slot], gr.at[slot], far(r)).wait_recv()

        def add(k, carry):
            cols = pl.ds(pl.multiple_of(k * tile, 128), tile)
            total = gw_ref[j, :, cols]
            for r in range(1, outer):
                total = total + grecv[(r - 1) * per + j, :, cols].astype(jnp.float32)
            gw_ref[j, :, cols] = total
            return carry
        lax.fori_loop(0, depth // tile, add, 0)

    for s in range(1, INNER):
        for r in range(outer):
            rdma(norm_buf.at[s, r], normed_ref.at[:, columns((o + r) % outer, inner_of(s))],
                 ns.at[s, r], nr.at[s, r], near(s)).wait_recv()
    for copy in keep:
        copy.wait()
    for copy in started:
        copy.wait_send()
    for wc in range(chunks):
        for q in range(1, tp):
            ag_copy(wc, q, t).wait_send()
        for s in range(INNER):
            for q in range(1, tp):
                rs_copy((t + q) % tp, wc, s, t).wait_send()


def body(dp, tp, hidden_states, fc_weight, norm_gain, upstream, lengths):
    tok_group, layers, slab = hidden_states.shape
    rows = fc_weight.shape[0]
    tok, draft = upstream.shape
    depth = layers * slab
    outer = dp // INNER
    chunk = min(256, rows)
    per = rows // chunk
    chunks = outer * per
    pieces = 2 if tp % 2 == 0 else 1
    bf, f32 = jnp.bfloat16, jnp.float32
    pos = lax.broadcasted_iota(jnp.int32, (tok, 1), 0)
    incoming = upstream * (pos < lengths[0]).astype(bf)
    dma = pltpu.SemaphoreType.DMA
    hbm = pl.BlockSpec(memory_space=pl.ANY)
    vmem = pl.BlockSpec(memory_space=pltpu.VMEM)
    flops = 4 * tok_group * draft * depth
    normed, gw, gg = pl.pallas_call(
        functools.partial(kernel, dp, tp, pieces),
        out_shape=(jax.ShapeDtypeStruct((tok, draft), bf),
                   jax.ShapeDtypeStruct((per, chunk, depth), f32),
                   jax.ShapeDtypeStruct((outer, INNER, per, 1, chunk), f32)),
        in_specs=[hbm, hbm, hbm, vmem],
        out_specs=(hbm, vmem, vmem),
        scratch_shapes=[
            pltpu.VMEM((tp, INNER, tok, depth), bf),
            pltpu.VMEM((chunks, chunk, depth), bf),
            pltpu.VMEM((chunks, tp, INNER, tok, chunk), bf),
            pltpu.VMEM((tp, chunks, INNER, tok, chunk), bf),
            pltpu.VMEM((INNER, chunks, tok, chunk), f32),
            pltpu.VMEM((INNER, outer, tok, rows), bf),
            pltpu.VMEM((INNER, outer, tok, rows), bf),
            pltpu.VMEM((chunks, tp, chunk, INNER * tok), bf),
            pltpu.VMEM((max(1, chunks - per), chunk, depth), bf),
            pltpu.VMEM((max(1, chunks - per), chunk, depth), bf),
            pltpu.VMEM((2 * INNER, tok), f32),
            pltpu.VMEM((INNER, 2 * INNER, tok), f32),
            pltpu.VMEM((chunks, chunk), f32),
            pltpu.VMEM((tp, chunks, chunk), f32),
            pltpu.VMEM((outer, chunks, chunk), f32),
            pltpu.VMEM((INNER, chunks, chunk), f32),
            dma((2 + outer,)),
            dma((3, pieces)), dma((INNER, pieces)),
            dma((chunks,)), dma((chunks,)),
            dma((INNER, outer)), dma((INNER, outer)),
            dma((tp, chunks, INNER)), dma((tp, chunks, INNER)),
            dma((INNER,)), dma((INNER,)),
            dma((chunks, tp)), dma((chunks, tp)),
            dma((INNER, outer)), dma((INNER, outer)),
            dma((chunks,)), dma((chunks,)),
            dma((tp,)), dma((tp,)),
            dma((outer,)), dma((outer,)),
            dma((INNER,)), dma((INNER,)),
        ],
        compiler_params=pltpu.CompilerParams(collective_id=0, has_side_effects=True,
                                             vmem_limit_bytes=62 * 2**20),
        cost_estimate=pl.CostEstimate(flops=flops, bytes_accessed=8 * tok_group * depth,
                                      transcendentals=0),
    )(hidden_states.reshape(tp, tok, depth), fc_weight.reshape(per, chunk, depth), incoming,
      norm_gain.reshape(outer, INNER, per, 1, chunk))
    return normed, gw.reshape(rows, layers, slab), gg.reshape(draft)


def solution(mesh):
    return jax.shard_map(
        functools.partial(body, mesh.shape["dp"], mesh.shape["tp"]),
        mesh=mesh,
        in_specs=(
            P("dp", None, "tp"),
            P("dp", None, "tp"),
            P(),
            P(("dp", "tp"), None),
            P(("dp", "tp")),
        ),
        out_specs=(P(("dp", "tp"), None), P("dp", None, "tp"), P()),
        check_vma=False,
    )
```

```python
import functools

import jax
import jax.numpy as jnp
from jax import lax
from jax.experimental import pallas as pl
from jax.experimental.pallas import tpu as pltpu
from jax.sharding import PartitionSpec as P

MESH = pl.DeviceIdType.MESH
INNER = 4


def kernel(dp, tp, h_ref, w_ref, up_ref, gain_ref, normed_ref, gw_ref, gg_ref,
           h_all, w_all, stage, parts, merged, up_all, norm_buf, gmt, gstage, grecv,
           st, st_all, gg, gg_tp, gg_out, gg_in,
           local_sem, hs, hr, ws, wr, us, ur, rs_s, rs_r, st_s, st_r, ag_s, ag_r,
           ns, nr, gs, gr, g1s, g1r, g2s, g2r, g3s, g3r):
    outer = dp // INNER
    d, t = lax.axis_index("dp"), lax.axis_index("tp")
    o, i = d // INNER, d % INNER
    x, c = i // 2, i % 2
    layers, _, tok, slab = h_ref.shape
    chunks, chunk = w_all.shape[1], w_all.shape[2]
    per = chunks // outer
    rows = per * chunk
    draft = dp * rows

    def inner_of(s):
        return ((x + s // 2) % 2) * 2 + (c + s % 2) % 2

    def near(s):
        return {"dp": o * INNER + inner_of(s)}

    def far(r):
        return {"dp": ((o + r) % outer) * INNER + i}

    def columns(block_o, block_i):
        return pl.ds(pl.multiple_of((block_o * INNER + block_i) * rows, 128), rows)

    def rdma(src, dst, ssem, rsem, dev):
        return pltpu.make_async_remote_copy(src_ref=src, dst_ref=dst, send_sem=ssem, recv_sem=rsem,
                                            device_id=dev, device_id_type=MESH)

    started = []

    def send(src, dst, ssem, rsem, dev):
        copy = rdma(src, dst, ssem, rsem, dev)
        copy.start()
        started.append(copy)

    mine = [pltpu.make_async_copy(h_ref, h_all.at[:, :, 0], local_sem.at[0]),
            pltpu.make_async_copy(w_ref, w_all.at[:, pl.ds(0, per)], local_sem.at[1])]
    for r in range(outer):
        mine.append(pltpu.make_async_copy(up_ref.at[:, columns((o + r) % outer, i)], up_all.at[0, r],
                                          local_sem.at[2 + r]))
    for copy in mine:
        copy.start()

    barrier = pltpu.get_barrier_semaphore()
    partners = ([near(s) for s in range(1, INNER)] + [far(r) for r in range(1, outer)]
                + [{"tp": (t + q) % tp} for q in range(1, tp)])
    for dev in partners:
        pl.semaphore_signal(barrier, inc=1, device_id=dev, device_id_type=MESH)
    pl.semaphore_wait(barrier, len(partners))

    def h_copy(p):
        return rdma(h_ref.at[:, p], h_all.at[:, p, 2], hs.at[0, p], hr.at[2, p], near(2))

    def own_copy(p):
        return rdma(h_ref.at[:, p], h_all.at[:, p, 1], hs.at[1, p], hr.at[1, p], near(1))

    def pass_copy(p):
        return rdma(h_all.at[:, p, 2], h_all.at[:, p, 3], hs.at[2, p], hr.at[3, p], near(1))

    def w_copy(m):
        wc, l = per + m // layers, m % layers
        r, j = outer - wc // per, wc % per
        return rdma(w_ref.at[l, j], w_all.at[l, wc], ws.at[m], wr.at[m], far(r))

    def go(copy):
        copy.start()
        started.append(copy)

    n_w = (chunks - per) * layers
    for p in range(min(2, tp)):
        go(h_copy(p))
    for m in range(min(2, n_w)):
        go(w_copy(m))
    for p in range(tp):
        go(own_copy(p))

    def rs_copy(z, wc, a, src):
        pair = pl.ds(2 * a, 2)
        return rdma(stage.at[wc, z, pair], parts.at[src, wc, pair], rs_s.at[z, wc, a],
                    rs_r.at[src, wc, a], {"tp": z})

    def product(z, a, wc):
        out = jnp.zeros((2 * tok, chunk), jnp.float32)
        for l in range(layers):
            left = h_all[l, z, 2 * a:2 * a + 2].reshape(2 * tok, slab)
            out = out + lax.dot_general(left, w_all[l, wc], (((1,), (1,)), ((), ())),
                                        preferred_element_type=jnp.float32)
        stage[wc, z, 2 * a:2 * a + 2] = out.astype(jnp.bfloat16).reshape(2, tok, chunk)

        @pl.when(t != z)
        def _():
            rs_copy(z, wc, a, t).start()

    def over(lo, hi, fn):
        def step(k, carry):
            fn(k)
            return carry
        lax.fori_loop(lo, hi, step, 0)

    mine[0].wait()
    mine[1].wait()
    for p in range(tp):
        own_copy(p).wait_recv()
    for wc in range(per):
        over(0, tp, lambda z: product((t + 1 + z) % tp, 0, wc))

    events = sorted([((p + 1) / tp, 1, p) for p in range(tp)]
                    + [((m + 1) / n_w, 0, m) for m in range(n_w)])
    have_w, have_h = per, 0
    for _, kind, n in events:
        if kind == 0:
            w_copy(n).wait_recv()
            if n + 2 < n_w:
                go(w_copy(n + 2))
            if n % layers == layers - 1:
                wc = have_w
                over(0, tp, lambda z: product((t + 1 + z) % tp, 0, wc))
                over(0, have_h, lambda z: product(z, 1, wc))
                have_w += 1
        else:
            h_copy(n).wait_recv()
            go(pass_copy(n))
            if n + 2 < tp:
                go(h_copy(n + 2))
            pass_copy(n).wait_recv()
            over(0, have_w, lambda wc: product(n, 1, wc))
            have_h += 1
            if have_h == tp:
                for s in range(1, INNER):
                    for r in range(outer):
                        send(up_ref.at[:, columns((o + r) % outer, inner_of(s))], up_all.at[s, r],
                             us.at[s, r], ur.at[s, r], near(s))

    for copy in mine[2:]:
        copy.wait()
    for s in range(1, INNER):
        for r in range(outer):
            rdma(up_ref.at[:, columns(o, i)], up_all.at[s, r], us.at[s, r], ur.at[s, r], near(s)).wait_recv()

    def gain_of(wc):
        r, j = wc // per, wc % per
        return gain_ref[(o + r) % outer, i, j]

    for s in range(INNER):
        sq = jnp.zeros((tok, 1), jnp.float32)
        al = jnp.zeros((tok, 1), jnp.float32)
        for wc in range(chunks):
            r, j = wc // per, wc % per
            total = stage[wc, t, s].astype(jnp.float32)
            for q in range(1, tp):
                src = (t + q) % tp
                if s % 2 == 0:
                    rs_copy(t, wc, s // 2, src).wait_recv()
                total = total + parts[src, wc, s].astype(jnp.float32)
            merged[s, wc] = total
            along = up_all[s, r, :, j * chunk:(j + 1) * chunk].astype(jnp.float32) * gain_of(wc)
            sq = sq + jnp.sum(total * total, axis=1, keepdims=True)
            al = al + jnp.sum(total * along, axis=1, keepdims=True)
        st[s:s + 1, :] = jnp.swapaxes(jnp.broadcast_to(sq, (tok, 128)), 0, 1)[0:1, :]
        st[INNER + s:INNER + s + 1, :] = jnp.swapaxes(jnp.broadcast_to(al, (tok, 128)), 0, 1)[0:1, :]
    for s in range(1, INNER):
        send(st, st_all.at[s], st_s.at[s], st_r.at[s], near(s))
    for s in range(1, INNER):
        rdma(st, st_all.at[s], st_s.at[s], st_r.at[s], near(s)).wait_recv()

    inverse, proj = [], []
    for s in range(INNER):
        sq, al = st[s:s + 1, :], st[INNER + s:INNER + s + 1, :]
        for q in range(1, INNER):
            k = ((s // 2 + q // 2) % 2) * 2 + (s + q) % 2
            sq = sq + st_all[q, k:k + 1, :]
            al = al + st_all[q, INNER + k:INNER + k + 1, :]
        inv = lax.rsqrt(sq / draft + 1e-05)
        pr = al * inv / draft
        inverse.append(jnp.swapaxes(jnp.broadcast_to(inv, (128, tok)), 0, 1)[:, 0:1])
        proj.append(jnp.swapaxes(jnp.broadcast_to(pr, (128, tok)), 0, 1)[:, 0:1])

    def ag_copy(wc, src, dr):
        side = (dr + 1) // 2
        return rdma(gmt.at[wc, src], gmt.at[wc, src], ag_s.at[wc, side, src],
                    ag_r.at[wc, side, src], {"tp": (t + dr + tp) % tp})

    def ag_own(wc):
        @pl.when(t < tp - 1)
        def _():
            ag_copy(wc, t, 1).start()

        @pl.when(t > 0)
        def _():
            ag_copy(wc, t, -1).start()

    def ag_take(wc):
        for k in range(1, tp):
            @pl.when(t - k >= 0)
            def _():
                ag_copy(wc, (t - k + tp) % tp, 1).wait_recv()

                @pl.when(t < tp - 1)
                def _():
                    ag_copy(wc, (t - k + tp) % tp, 1).start()

            @pl.when(t + k < tp)
            def _():
                ag_copy(wc, (t + k) % tp, -1).wait_recv()

                @pl.when(t > 0)
                def _():
                    ag_copy(wc, (t + k) % tp, -1).start()

    def ag_done(wc):
        for k in range(tp):
            @pl.when((t - k >= 0) & (t < tp - 1))
            def _():
                ag_copy(wc, (t - k + tp) % tp, 1).wait_send()

            @pl.when((t + k < tp) & (t > 0))
            def _():
                ag_copy(wc, (t + k) % tp, -1).wait_send()

    order = list(range(per, chunks)) + list(range(per))
    for wc in order:
        r, j = wc // per, wc % per
        gain = gain_of(wc)
        own = jnp.zeros((1, chunk), jnp.float32)
        for s in range(INNER):
            scaled = merged[s, wc] * inverse[s]
            incoming = up_all[s, r, :, j * chunk:(j + 1) * chunk].astype(jnp.float32)
            norm_buf[s, r, :, j * chunk:(j + 1) * chunk] = (scaled * gain).astype(jnp.bfloat16)
            own = own + jnp.sum(incoming * scaled, axis=0, keepdims=True)
            grad = inverse[s] * (incoming * gain - scaled * proj[s])
            gmt[wc, t, :, s * tok:(s + 1) * tok] = jnp.swapaxes(grad, 0, 1).astype(jnp.bfloat16)
        gg[wc:wc + 1, :] = own
        if wc in order[:2]:
            ag_own(wc)

    for s in range(1, INNER):
        for r in range(outer):
            send(norm_buf.at[s, r], normed_ref.at[:, columns((o + r) % outer, i)],
                 ns.at[s, r], nr.at[s, r], near(s))
    keep = []
    for r in range(outer):
        copy = pltpu.make_async_copy(norm_buf.at[0, r], normed_ref.at[:, columns((o + r) % outer, i)],
                                     local_sem.at[2 + r])
        copy.start()
        keep.append(copy)
    for q in range(1, tp):
        send(gg, gg_tp.at[tp - q], g1s.at[q], g1r.at[tp - q], {"tp": (t + q) % tp})

    def gain_step(n):
        if n == 0:
            total = gg[...]
            for q in range(1, tp):
                rdma(gg, gg_tp.at[q], g1s.at[q], g1r.at[q], {"tp": (t + q) % tp}).wait_recv()
                total = total + gg_tp[q]
            gg_out[0] = total
            for r in range(1, outer):
                send(gg_out.at[0], gg_out.at[outer - r], g2s.at[r], g2r.at[outer - r], far(r))
        if n == 1:
            for r in range(1, outer):
                rdma(gg_out.at[0], gg_out.at[r], g2s.at[r], g2r.at[r], far(r)).wait_recv()
            for wc in range(chunks):
                total = gg_out[0, wc:wc + 1, :]
                for r in range(1, outer):
                    k = (wc - r * per) % chunks
                    total = total + gg_out[r, k:k + 1, :]
                gg_in[0, wc:wc + 1, :] = total
            for s in range(1, INNER):
                send(gg_in.at[0], gg_in.at[s], g3s.at[s], g3r.at[s], near(s))
        if n == 2:
            for s in range(1, INNER):
                rdma(gg_in.at[0], gg_in.at[s], g3s.at[s], g3r.at[s], near(s)).wait_recv()
            for s in range(INNER):
                for wc in range(chunks):
                    gg_ref[(o + wc // per) % outer, inner_of(s), wc % per] = gg_in[s, wc:wc + 1, :]

    tile = min(512, slab)

    def g_copy(k, l, r):
        slot = (outer - r - 1) * per + k % per
        return rdma(gstage.at[k, l], grecv.at[slot, l], gs.at[slot, l], gr.at[slot, l], far(r))

    for n, wc in enumerate(order):
        ag_take(wc)
        if n + 2 < chunks:
            ag_own(order[n + 2])
        for l in range(layers):
            def step(k, carry):
                cols = pl.ds(pl.multiple_of(k * tile, 128), tile)
                acc = jnp.zeros((chunk, tile), jnp.float32)
                for z in range(tp):
                    right = h_all[l, z, :, :, cols].reshape(INNER * tok, tile)
                    acc = acc + jnp.dot(gmt[wc, z], right, preferred_element_type=jnp.float32)
                if wc >= per:
                    gstage[wc - per, l, :, cols] = acc.astype(jnp.bfloat16)
                else:
                    gw_ref[l, wc, :, cols] = acc
                return carry
            lax.fori_loop(0, slab // tile, step, 0)
            if wc >= per:
                go(g_copy(wc - per, l, wc // per))
        gain_step(n)
    for j in range(per):
        for l in range(layers):
            for r in range(1, outer):
                slot = (r - 1) * per + j
                rdma(gstage.at[0, l], grecv.at[slot, l], gs.at[slot, l], gr.at[slot, l], far(r)).wait_recv()

            def add(k, carry):
                cols = pl.ds(pl.multiple_of(k * tile, 128), tile)
                total = gw_ref[l, j, :, cols]
                for r in range(1, outer):
                    total = total + grecv[(r - 1) * per + j, l, :, cols].astype(jnp.float32)
                gw_ref[l, j, :, cols] = total
                return carry
            lax.fori_loop(0, slab // tile, add, 0)

    for s in range(1, INNER):
        for r in range(outer):
            rdma(norm_buf.at[s, r], normed_ref.at[:, columns((o + r) % outer, inner_of(s))],
                 ns.at[s, r], nr.at[s, r], near(s)).wait_recv()
    for copy in keep:
        copy.wait()
    for copy in started:
        copy.wait_send()
    for wc in range(chunks):
        ag_done(wc)
        for a in range(INNER // 2):
            for q in range(1, tp):
                rs_copy((t + q) % tp, wc, a, t).wait_send()


def body(dp, tp, hidden_states, fc_weight, norm_gain, upstream, lengths):
    tok_group, layers, slab = hidden_states.shape
    rows = fc_weight.shape[0]
    tok, draft = upstream.shape
    depth = layers * slab
    outer = dp // INNER
    chunk = min(256, rows)
    per = rows // chunk
    chunks = outer * per
    bf, f32 = jnp.bfloat16, jnp.float32
    pos = lax.broadcasted_iota(jnp.int32, (tok, 1), 0)
    incoming = upstream * (pos < lengths[0]).astype(bf)
    dma = pltpu.SemaphoreType.DMA
    hbm = pl.BlockSpec(memory_space=pl.ANY)
    vmem = pl.BlockSpec(memory_space=pltpu.VMEM)
    flops = 4 * tok_group * draft * depth
    normed, gw, gg = pl.pallas_call(
        functools.partial(kernel, dp, tp),
        out_shape=(jax.ShapeDtypeStruct((tok, draft), bf),
                   jax.ShapeDtypeStruct((layers, per, chunk, slab), f32),
                   jax.ShapeDtypeStruct((outer, INNER, per, 1, chunk), f32)),
        in_specs=[hbm, hbm, hbm, vmem],
        out_specs=(hbm, vmem, vmem),
        scratch_shapes=[
            pltpu.VMEM((layers, tp, INNER, tok, slab), bf),
            pltpu.VMEM((layers, chunks, chunk, slab), bf),
            pltpu.VMEM((chunks, tp, INNER, tok, chunk), bf),
            pltpu.VMEM((tp, chunks, INNER, tok, chunk), bf),
            pltpu.VMEM((INNER, chunks, tok, chunk), f32),
            pltpu.VMEM((INNER, outer, tok, rows), bf),
            pltpu.VMEM((INNER, outer, tok, rows), bf),
            pltpu.VMEM((chunks, tp, chunk, INNER * tok), bf),
            pltpu.VMEM((max(1, chunks - per), layers, chunk, slab), bf),
            pltpu.VMEM((max(1, chunks - per), layers, chunk, slab), bf),
            pltpu.VMEM((2 * INNER, tok), f32),
            pltpu.VMEM((INNER, 2 * INNER, tok), f32),
            pltpu.VMEM((chunks, chunk), f32),
            pltpu.VMEM((tp, chunks, chunk), f32),
            pltpu.VMEM((outer, chunks, chunk), f32),
            pltpu.VMEM((INNER, chunks, chunk), f32),
            dma((2 + outer,)),
            dma((3, tp)), dma((INNER, tp)),
            dma((chunks * layers,)), dma((chunks * layers,)),
            dma((INNER, outer)), dma((INNER, outer)),
            dma((tp, chunks, INNER // 2)), dma((tp, chunks, INNER // 2)),
            dma((INNER,)), dma((INNER,)),
            dma((chunks, 2, tp)), dma((chunks, 2, tp)),
            dma((INNER, outer)), dma((INNER, outer)),
            dma((chunks, layers)), dma((chunks, layers)),
            dma((tp,)), dma((tp,)),
            dma((outer,)), dma((outer,)),
            dma((INNER,)), dma((INNER,)),
        ],
        compiler_params=pltpu.CompilerParams(collective_id=0, has_side_effects=True,
                                             vmem_limit_bytes=62 * 2**20),
        cost_estimate=pl.CostEstimate(flops=flops, bytes_accessed=8 * tok_group * depth,
                                      transcendentals=0),
    )(hidden_states.transpose(1, 0, 2).reshape(layers, tp, tok, slab),
      fc_weight.transpose(1, 0, 2).reshape(layers, per, chunk, slab), incoming,
      norm_gain.reshape(outer, INNER, per, 1, chunk))
    return normed, gw.reshape(layers, rows, slab).transpose(1, 0, 2), gg.reshape(draft)


def solution(mesh):
    return jax.shard_map(
        functools.partial(body, mesh.shape["dp"], mesh.shape["tp"]),
        mesh=mesh,
        in_specs=(
            P("dp", None, "tp"),
            P("dp", None, "tp"),
            P(),
            P(("dp", "tp"), None),
            P(("dp", "tp")),
        ),
        out_specs=(P(("dp", "tp"), None), P("dp", None, "tp"), P()),
        check_vma=False,
    )
```

```python
import functools

import jax
import jax.numpy as jnp
from jax import lax
from jax.experimental import pallas as pl
from jax.experimental.pallas import tpu as pltpu
from jax.sharding import PartitionSpec as P

MESH = pl.DeviceIdType.MESH
INNER = 4


def kernel(dp, tp, h_ref, w_ref, up_ref, gain_ref, len_ref, normed_ref, gown_ref, grecv, gg_ref,
           h_all, w_all, stage, parts, merged, up_all, norm_buf, gmt, gstage, gown, up_v,
           st, st_all, gg, gg_tp, gg_out, gg_in,
           local_sem, hs, hr, ws, wr, us, ur, rs_s, rs_r, st_s, st_r, ag_s, ag_r,
           ns, nr, gs, gr, go_s, g1s, g1r, g2s, g2r, g3s, g3r):
    outer = dp // INNER
    d, t = lax.axis_index("dp"), lax.axis_index("tp")
    o, i = d // INNER, d % INNER
    x, c = i // 2, i % 2
    layers, _, tok, slab = h_ref.shape
    chunks, chunk = w_all.shape[1], w_all.shape[2]
    per = chunks // outer
    rows = per * chunk
    part = gmt.shape[2]
    split = chunk // part
    per_g = per * split
    parts_g = chunks * split
    draft = dp * rows

    def inner_of(s):
        return ((x + s // 2) % 2) * 2 + (c + s % 2) % 2

    def near(s):
        return {"dp": o * INNER + inner_of(s)}

    def far(r):
        return {"dp": ((o + r) % outer) * INNER + i}

    def columns(block_o, block_i):
        return pl.ds(pl.multiple_of((block_o * INNER + block_i) * rows, 128), rows)

    def rdma(src, dst, ssem, rsem, dev):
        return pltpu.make_async_remote_copy(src_ref=src, dst_ref=dst, send_sem=ssem, recv_sem=rsem,
                                            device_id=dev, device_id_type=MESH)

    started = []

    def send(src, dst, ssem, rsem, dev):
        copy = rdma(src, dst, ssem, rsem, dev)
        copy.start()
        started.append(copy)

    mine = [pltpu.make_async_copy(h_ref, h_all.at[:, :, 0], local_sem.at[0]),
            pltpu.make_async_copy(w_ref, w_all.at[:, pl.ds(0, per)], local_sem.at[1])]
    mine.append(pltpu.make_async_copy(up_ref, up_v, local_sem.at[2]))
    for copy in mine:
        copy.start()

    barrier = pltpu.get_barrier_semaphore()
    partners = ([near(s) for s in range(1, INNER)] + [far(r) for r in range(1, outer)]
                + [{"tp": (t + q) % tp} for q in range(1, tp)])
    for dev in partners:
        pl.semaphore_signal(barrier, inc=1, device_id=dev, device_id_type=MESH)
    pl.semaphore_wait(barrier, len(partners))

    def h_copy(p):
        return rdma(h_ref.at[:, p], h_all.at[:, p, 2], hs.at[0, p], hr.at[2, p], near(2))

    def own_copy(p):
        return rdma(h_ref.at[:, p], h_all.at[:, p, 1], hs.at[1, p], hr.at[1, p], near(1))

    def pass_copy(p):
        return rdma(h_all.at[:, p, 2], h_all.at[:, p, 3], hs.at[2, p], hr.at[3, p], near(1))

    def w_copy(m):
        wc, l = per + m // layers, m % layers
        r, j = outer - wc // per, wc % per
        return rdma(w_ref.at[l, j], w_all.at[l, wc], ws.at[m], wr.at[m], far(r))

    def go(copy):
        copy.start()
        started.append(copy)

    n_w = (chunks - per) * layers
    for p in range(min(2, tp)):
        go(h_copy(p))
    for m in range(min(2, n_w)):
        go(w_copy(m))
    for p in range(tp):
        go(own_copy(p))

    def rs_copy(z, wc, a, src):
        pair = pl.ds(2 * a, 2)
        return rdma(stage.at[wc, z, pair], parts.at[src, wc, pair], rs_s.at[z, wc, a],
                    rs_r.at[src, wc, a], {"tp": z})

    def product(z, a, wc):
        out = jnp.zeros((2 * tok, chunk), jnp.float32)
        for l in range(layers):
            left = h_all[l, z, 2 * a:2 * a + 2].reshape(2 * tok, slab)
            out = out + lax.dot_general(left, w_all[l, wc], (((1,), (1,)), ((), ())),
                                        preferred_element_type=jnp.float32)
        stage[wc, z, 2 * a:2 * a + 2] = out.astype(jnp.bfloat16).reshape(2, tok, chunk)

        @pl.when(t != z)
        def _():
            rs_copy(z, wc, a, t).start()

    def over(lo, hi, fn):
        def step(k, carry):
            fn(k)
            return carry
        lax.fori_loop(lo, hi, step, 0)

    mine[0].wait()
    mine[1].wait()
    mine[2].wait()
    live = (lax.broadcasted_iota(jnp.int32, (tok, 1), 0) < len_ref[0]).astype(jnp.float32)
    for p in range(tp):
        own_copy(p).wait_recv()
    for wc in range(per):
        over(0, tp, lambda z: product((t + 1 + z) % tp, 0, wc))

    def mask(k):
        cols = pl.ds(pl.multiple_of(k * rows, 128), rows)
        up_v[:, cols] = (up_v[:, cols].astype(jnp.float32) * live).astype(jnp.bfloat16)
    over(0, dp, mask)
    local = [pltpu.make_async_copy(up_v.at[:, columns((o + r) % outer, i)], up_all.at[0, r],
                                   local_sem.at[2 + r]) for r in range(outer)]
    for copy in local:
        copy.start()

    events = sorted([((p + 1) / tp, 1, p) for p in range(tp)]
                    + [((m + 1) / n_w, 0, m) for m in range(n_w)])
    have_w, have_h = per, 0
    for _, kind, n in events:
        if kind == 0:
            w_copy(n).wait_recv()
            if n + 2 < n_w:
                go(w_copy(n + 2))
            if n % layers == layers - 1:
                wc = have_w
                over(0, tp, lambda z: product((t + 1 + z) % tp, 0, wc))
                over(0, have_h, lambda z: product(z, 1, wc))
                have_w += 1
        else:
            h_copy(n).wait_recv()
            go(pass_copy(n))
            if n + 2 < tp:
                go(h_copy(n + 2))
            pass_copy(n).wait_recv()
            over(0, have_w, lambda wc: product(n, 1, wc))
            have_h += 1
            if have_h == tp:
                for s in range(1, INNER):
                    for r in range(outer):
                        send(up_v.at[:, columns((o + r) % outer, inner_of(s))], up_all.at[s, r],
                             us.at[s, r], ur.at[s, r], near(s))

    for copy in local:
        copy.wait()
    for s in range(1, INNER):
        for r in range(outer):
            rdma(up_v.at[:, columns(o, i)], up_all.at[s, r], us.at[s, r], ur.at[s, r], near(s)).wait_recv()

    def gain_of(wc):
        r, j = wc // per, wc % per
        return gain_ref[(o + r) % outer, i, j]

    for s in range(INNER):
        sq = jnp.zeros((tok, 1), jnp.float32)
        al = jnp.zeros((tok, 1), jnp.float32)
        for wc in range(chunks):
            r, j = wc // per, wc % per
            total = stage[wc, t, s].astype(jnp.float32)
            for q in range(1, tp):
                src = (t + q) % tp
                if s % 2 == 0:
                    rs_copy(t, wc, s // 2, src).wait_recv()
                total = total + parts[src, wc, s].astype(jnp.float32)
            merged[s, wc] = total
            along = up_all[s, r, :, j * chunk:(j + 1) * chunk].astype(jnp.float32) * gain_of(wc)
            sq = sq + jnp.sum(total * total, axis=1, keepdims=True)
            al = al + jnp.sum(total * along, axis=1, keepdims=True)
        st[s:s + 1, :] = jnp.swapaxes(jnp.broadcast_to(sq, (tok, 128)), 0, 1)[0:1, :]
        st[INNER + s:INNER + s + 1, :] = jnp.swapaxes(jnp.broadcast_to(al, (tok, 128)), 0, 1)[0:1, :]
    for s in range(1, INNER):
        send(st, st_all.at[s], st_s.at[s], st_r.at[s], near(s))
    for s in range(1, INNER):
        rdma(st, st_all.at[s], st_s.at[s], st_r.at[s], near(s)).wait_recv()

    inverse, proj = [], []
    for s in range(INNER):
        sq, al = st[s:s + 1, :], st[INNER + s:INNER + s + 1, :]
        for q in range(1, INNER):
            k = ((s // 2 + q // 2) % 2) * 2 + (s + q) % 2
            sq = sq + st_all[q, k:k + 1, :]
            al = al + st_all[q, INNER + k:INNER + k + 1, :]
        inv = lax.rsqrt(sq / draft + 1e-05)
        pr = al * inv / draft
        inverse.append(jnp.swapaxes(jnp.broadcast_to(inv, (128, tok)), 0, 1)[:, 0:1])
        proj.append(jnp.swapaxes(jnp.broadcast_to(pr, (128, tok)), 0, 1)[:, 0:1])

    def ag_copy(wc, src, dr):
        side = (dr + 1) // 2
        return rdma(gmt.at[wc, src], gmt.at[wc, src], ag_s.at[wc, side, src],
                    ag_r.at[wc, side, src], {"tp": (t + dr + tp) % tp})

    def ag_own(wc):
        @pl.when(t < tp - 1)
        def _():
            ag_copy(wc, t, 1).start()

        @pl.when(t > 0)
        def _():
            ag_copy(wc, t, -1).start()

    def ag_take(wc):
        for k in range(1, tp):
            @pl.when(t - k >= 0)
            def _():
                ag_copy(wc, (t - k + tp) % tp, 1).wait_recv()

                @pl.when(t < tp - 1)
                def _():
                    ag_copy(wc, (t - k + tp) % tp, 1).start()

            @pl.when(t + k < tp)
            def _():
                ag_copy(wc, (t + k) % tp, -1).wait_recv()

                @pl.when(t > 0)
                def _():
                    ag_copy(wc, (t + k) % tp, -1).start()

    def ag_done(wc):
        for k in range(tp):
            @pl.when((t - k >= 0) & (t < tp - 1))
            def _():
                ag_copy(wc, (t - k + tp) % tp, 1).wait_send()

            @pl.when((t + k < tp) & (t > 0))
            def _():
                ag_copy(wc, (t + k) % tp, -1).wait_send()

    order = list(range(per_g, parts_g)) + list(range(per_g))
    for g in order:
        r, j, wc = g // per_g, g % per_g, g // split
        here = slice(j * part, (j + 1) * part)
        sub = slice((g % split) * part, (g % split + 1) * part)
        gain = gain_of(wc)[:, sub]
        own = jnp.zeros((1, part), jnp.float32)
        for s in range(INNER):
            scaled = merged[s, wc, :, sub] * inverse[s]
            incoming = up_all[s, r, :, here].astype(jnp.float32)
            norm_buf[s, r, :, here] = (scaled * gain).astype(jnp.bfloat16)
            own = own + jnp.sum(incoming * scaled, axis=0, keepdims=True)
            grad = inverse[s] * (incoming * gain - scaled * proj[s])
            gmt[g, t, :, s * tok:(s + 1) * tok] = jnp.swapaxes(grad, 0, 1).astype(jnp.bfloat16)
        gg[wc:wc + 1, sub] = own
        if g in order[:2]:
            ag_own(g)

    for s in range(1, INNER):
        for r in range(outer):
            send(norm_buf.at[s, r], normed_ref.at[:, columns((o + r) % outer, i)],
                 ns.at[s, r], nr.at[s, r], near(s))
    keep = []
    for r in range(outer):
        copy = pltpu.make_async_copy(norm_buf.at[0, r], normed_ref.at[:, columns((o + r) % outer, i)],
                                     local_sem.at[2 + r])
        copy.start()
        keep.append(copy)
    for q in range(1, tp):
        send(gg, gg_tp.at[tp - q], g1s.at[q], g1r.at[tp - q], {"tp": (t + q) % tp})

    def gain_step(n):
        if n == 0:
            total = gg[...]
            for q in range(1, tp):
                rdma(gg, gg_tp.at[q], g1s.at[q], g1r.at[q], {"tp": (t + q) % tp}).wait_recv()
                total = total + gg_tp[q]
            gg_out[0] = total
            for r in range(1, outer):
                send(gg_out.at[0], gg_out.at[outer - r], g2s.at[r], g2r.at[outer - r], far(r))
        if n == 1:
            for r in range(1, outer):
                rdma(gg_out.at[0], gg_out.at[r], g2s.at[r], g2r.at[r], far(r)).wait_recv()
            for wc in range(chunks):
                total = gg_out[0, wc:wc + 1, :]
                for r in range(1, outer):
                    k = (wc - r * per) % chunks
                    total = total + gg_out[r, k:k + 1, :]
                gg_in[0, wc:wc + 1, :] = total
            for s in range(1, INNER):
                send(gg_in.at[0], gg_in.at[s], g3s.at[s], g3r.at[s], near(s))
        if n == 2:
            for s in range(1, INNER):
                rdma(gg_in.at[0], gg_in.at[s], g3s.at[s], g3r.at[s], near(s)).wait_recv()
            for s in range(INNER):
                for wc in range(chunks):
                    gg_ref[(o + wc // per) % outer, inner_of(s), wc % per] = gg_in[s, wc:wc + 1, :]

    tile = min(512, slab)

    def g_copy(k, l, r):
        return rdma(gstage.at[k, l], grecv.at[outer - r - 1, l, k % per_g], gs.at[k, l],
                    gr.at[outer - r - 1, l, k % per_g], far(r))

    for n, g in enumerate(order):
        ag_take(g)
        if n + 2 < parts_g:
            ag_own(order[n + 2])
        for l in range(layers):
            def step(k, carry):
                cols = pl.ds(pl.multiple_of(k * tile, 128), tile)
                acc = jnp.zeros((part, tile), jnp.float32)
                for z in range(tp):
                    right = h_all[l, z, :, :, cols].reshape(INNER * tok, tile)
                    acc = acc + jnp.dot(gmt[g, z], right, preferred_element_type=jnp.float32)
                if g >= per_g:
                    gstage[g - per_g, l, :, cols] = acc.astype(jnp.bfloat16)
                else:
                    gown[l, g, :, cols] = acc.astype(jnp.bfloat16)
                return carry
            lax.fori_loop(0, slab // tile, step, 0)
            if g >= per_g:
                go(g_copy(g - per_g, l, g // per_g))
            else:
                copy = pltpu.make_async_copy(gown.at[l, g], gown_ref.at[l, g], go_s.at[l, g])
                copy.start()
                keep.append(copy)
        if n % 2 == 1:
            gain_step(n // 2)
    for r in range(1, outer):
        for j in range(per_g):
            for l in range(layers):
                rdma(gstage.at[0, l], grecv.at[r - 1, l, j], gs.at[j, l], gr.at[r - 1, l, j], far(r)).wait_recv()

    for s in range(1, INNER):
        for r in range(outer):
            rdma(norm_buf.at[s, r], normed_ref.at[:, columns((o + r) % outer, inner_of(s))],
                 ns.at[s, r], nr.at[s, r], near(s)).wait_recv()
    for copy in keep:
        copy.wait()
    for copy in started:
        copy.wait_send()
    for g in range(parts_g):
        ag_done(g)
    for wc in range(chunks):
        for a in range(INNER // 2):
            for q in range(1, tp):
                rs_copy((t + q) % tp, wc, a, t).wait_send()


def body(dp, tp, hidden_states, fc_weight, norm_gain, upstream, lengths):
    tok_group, layers, slab = hidden_states.shape
    rows = fc_weight.shape[0]
    tok, draft = upstream.shape
    depth = layers * slab
    outer = dp // INNER
    chunk = min(256, rows)
    per = rows // chunk
    chunks = outer * per
    bf, f32 = jnp.bfloat16, jnp.float32
    part = min(128, chunk)
    parts_g, per_g = rows * outer // part, rows // part
    dma = pltpu.SemaphoreType.DMA
    hbm = pl.BlockSpec(memory_space=pl.ANY)
    vmem = pl.BlockSpec(memory_space=pltpu.VMEM)
    flops = 4 * tok_group * draft * depth
    normed, own, others, gg = pl.pallas_call(
        functools.partial(kernel, dp, tp),
        out_shape=(jax.ShapeDtypeStruct((tok, draft), bf),
                   jax.ShapeDtypeStruct((layers, per_g, part, slab), bf),
                   jax.ShapeDtypeStruct((max(1, outer - 1), layers, per_g, part, slab), bf),
                   jax.ShapeDtypeStruct((outer, INNER, per, 1, chunk), f32)),
        in_specs=[hbm, hbm, hbm, vmem, pl.BlockSpec(memory_space=pltpu.SMEM)],
        out_specs=(hbm, hbm, hbm, vmem),
        scratch_shapes=[
            pltpu.VMEM((layers, tp, INNER, tok, slab), bf),
            pltpu.VMEM((layers, chunks, chunk, slab), bf),
            pltpu.VMEM((chunks, tp, INNER, tok, chunk), bf),
            pltpu.VMEM((tp, chunks, INNER, tok, chunk), bf),
            pltpu.VMEM((INNER, chunks, tok, chunk), f32),
            pltpu.VMEM((INNER, outer, tok, rows), bf),
            pltpu.VMEM((INNER, outer, tok, rows), bf),
            pltpu.VMEM((parts_g, tp, part, INNER * tok), bf),
            pltpu.VMEM((max(1, parts_g - per_g), layers, part, slab), bf),
            pltpu.VMEM((layers, per_g, part, slab), bf),
            pltpu.VMEM((tok, draft), bf),
            pltpu.VMEM((2 * INNER, tok), f32),
            pltpu.VMEM((INNER, 2 * INNER, tok), f32),
            pltpu.VMEM((chunks, chunk), f32),
            pltpu.VMEM((tp, chunks, chunk), f32),
            pltpu.VMEM((outer, chunks, chunk), f32),
            pltpu.VMEM((INNER, chunks, chunk), f32),
            dma((2 + outer,)),
            dma((3, tp)), dma((INNER, tp)),
            dma((chunks * layers,)), dma((chunks * layers,)),
            dma((INNER, outer)), dma((INNER, outer)),
            dma((tp, chunks, INNER // 2)), dma((tp, chunks, INNER // 2)),
            dma((INNER,)), dma((INNER,)),
            dma((parts_g, 2, tp)), dma((parts_g, 2, tp)),
            dma((INNER, outer)), dma((INNER, outer)),
            dma((max(1, parts_g - per_g), layers)), dma((max(1, outer - 1), layers, per_g)),
            dma((layers, per_g)),
            dma((tp,)), dma((tp,)),
            dma((outer,)), dma((outer,)),
            dma((INNER,)), dma((INNER,)),
        ],
        compiler_params=pltpu.CompilerParams(collective_id=0, has_side_effects=True,
                                             vmem_limit_bytes=62 * 2**20),
        cost_estimate=pl.CostEstimate(flops=flops, bytes_accessed=8 * tok_group * depth,
                                      transcendentals=0),
    )(hidden_states.transpose(1, 0, 2).reshape(layers, tp, tok, slab),
      fc_weight.transpose(1, 0, 2).reshape(layers, per, chunk, slab), upstream,
      norm_gain.reshape(outer, INNER, per, 1, chunk), lengths)
    gw = own.astype(f32)
    for r in range(outer - 1):
        gw = gw + others[r].astype(f32)
    return normed, gw.reshape(layers, rows, slab).transpose(1, 0, 2), gg.reshape(draft)


def solution(mesh):
    return jax.shard_map(
        functools.partial(body, mesh.shape["dp"], mesh.shape["tp"]),
        mesh=mesh,
        in_specs=(
            P("dp", None, "tp"),
            P("dp", None, "tp"),
            P(),
            P(("dp", "tp"), None),
            P(("dp", "tp")),
        ),
        out_specs=(P(("dp", "tp"), None), P("dp", None, "tp"), P()),
        check_vma=False,
    )
```

```python
import functools

import jax
import jax.numpy as jnp
from jax import lax
from jax.experimental import pallas as pl
from jax.experimental.pallas import tpu as pltpu
from jax.sharding import PartitionSpec as P

MESH = pl.DeviceIdType.MESH
INNER = 4


def kernel(dp, tp, h_ref, w_ref, up_ref, gain_ref, len_ref, normed_ref, gown_ref, grecv, gg_ref,
           h_all, w_all, stage, parts, merged, up_all, norm_buf, gmt, gstage, gown, up_v,
           st, st_all, gg, gg_tp, gg_out, gg_in,
           local_sem, hs, hr, ws, wr, us, ur, rs_s, rs_r, st_s, st_r, ag_s, ag_r,
           ns, nr, gs, gr, go_s, g1s, g1r, g2s, g2r, g3s, g3r):
    outer = dp // INNER
    d, t = lax.axis_index("dp"), lax.axis_index("tp")
    o, i = d // INNER, d % INNER
    x, c = i // 2, i % 2
    layers, _, tok, slab = h_ref.shape
    chunks, chunk = w_all.shape[1], w_all.shape[2]
    per = chunks // outer
    rows = per * chunk
    part = gmt.shape[2]
    split = chunk // part
    per_g = per * split
    parts_g = chunks * split
    draft = dp * rows

    def inner_of(s):
        return ((x + s // 2) % 2) * 2 + (c + s % 2) % 2

    def near(s):
        return {"dp": o * INNER + inner_of(s)}

    def far(r):
        return {"dp": ((o + r) % outer) * INNER + i}

    def columns(block_o, block_i):
        return pl.ds(pl.multiple_of((block_o * INNER + block_i) * rows, 128), rows)

    def rdma(src, dst, ssem, rsem, dev):
        return pltpu.make_async_remote_copy(src_ref=src, dst_ref=dst, send_sem=ssem, recv_sem=rsem,
                                            device_id=dev, device_id_type=MESH)

    started = []

    def send(src, dst, ssem, rsem, dev):
        copy = rdma(src, dst, ssem, rsem, dev)
        copy.start()
        started.append(copy)

    mine = [pltpu.make_async_copy(h_ref, h_all.at[:, :, 0], local_sem.at[0]),
            pltpu.make_async_copy(w_ref, w_all.at[:, pl.ds(0, per)], local_sem.at[1])]
    mine.append(pltpu.make_async_copy(up_ref, up_v, local_sem.at[2]))
    for copy in mine:
        copy.start()

    barrier = pltpu.get_barrier_semaphore()
    partners = ([near(s) for s in range(1, INNER)] + [far(r) for r in range(1, outer)]
                + [{"tp": (t + q) % tp} for q in range(1, tp)])
    for dev in partners:
        pl.semaphore_signal(barrier, inc=1, device_id=dev, device_id_type=MESH)
    pl.semaphore_wait(barrier, len(partners))

    def h_copy(p):
        return rdma(h_ref.at[:, p], h_all.at[:, p, 2], hs.at[0, p], hr.at[2, p], near(2))

    def own_copy(p):
        return rdma(h_ref.at[:, p], h_all.at[:, p, 1], hs.at[1, p], hr.at[1, p], near(1))

    def pass_copy(p):
        return rdma(h_all.at[:, p, 2], h_all.at[:, p, 3], hs.at[2, p], hr.at[3, p], near(1))

    def w_copy(m):
        wc, l = per + m // layers, m % layers
        r, j = outer - wc // per, wc % per
        return rdma(w_ref.at[l, j], w_all.at[l, wc], ws.at[m], wr.at[m], far(r))

    def go(copy):
        copy.start()
        started.append(copy)

    n_w = (chunks - per) * layers
    for p in range(min(2, tp)):
        go(h_copy(p))
    for m in range(min(2, n_w)):
        go(w_copy(m))
    for p in range(tp):
        go(own_copy(p))

    def rs_copy(z, wc, a, src):
        pair = pl.ds(2 * a, 2)
        return rdma(stage.at[wc, z, pair], parts.at[src, wc, pair], rs_s.at[z, wc, a],
                    rs_r.at[src, wc, a], {"tp": z})

    def product(z, a, wc):
        out = jnp.zeros((2 * tok, chunk), jnp.float32)
        for l in range(layers):
            left = h_all[l, z, 2 * a:2 * a + 2].reshape(2 * tok, slab)
            out = out + lax.dot_general(left, w_all[l, wc], (((1,), (1,)), ((), ())),
                                        preferred_element_type=jnp.float32)
        stage[wc, z, 2 * a:2 * a + 2] = out.astype(jnp.bfloat16).reshape(2, tok, chunk)

        @pl.when(t != z)
        def _():
            rs_copy(z, wc, a, t).start()

    def over(lo, hi, fn):
        def step(k, carry):
            fn(k)
            return carry
        lax.fori_loop(lo, hi, step, 0)

    mine[0].wait()
    mine[1].wait()
    mine[2].wait()
    live = (lax.broadcasted_iota(jnp.int32, (tok, 1), 0) < len_ref[0]).astype(jnp.float32)
    for p in range(tp):
        own_copy(p).wait_recv()
    for wc in range(per):
        over(0, tp, lambda z: product((t + 1 + z) % tp, 0, wc))

    def mask(k):
        cols = pl.ds(pl.multiple_of(k * rows, 128), rows)
        up_v[:, cols] = (up_v[:, cols].astype(jnp.float32) * live).astype(jnp.bfloat16)
    over(0, dp, mask)
    local = [pltpu.make_async_copy(up_v.at[:, columns((o + r) % outer, i)], up_all.at[0, r],
                                   local_sem.at[2 + r]) for r in range(outer)]
    for copy in local:
        copy.start()

    events = sorted([((p + 1) / tp, 1, p) for p in range(tp)]
                    + [((m + 1) / n_w, 0, m) for m in range(n_w)])
    have_w, have_h = per, 0
    for _, kind, n in events:
        if kind == 0:
            w_copy(n).wait_recv()
            if n + 2 < n_w:
                go(w_copy(n + 2))
            if n % layers == layers - 1:
                wc = have_w
                over(0, tp, lambda z: product((t + 1 + z) % tp, 0, wc))
                over(0, have_h, lambda z: product(z, 1, wc))
                have_w += 1
        else:
            h_copy(n).wait_recv()
            go(pass_copy(n))
            if n + 2 < tp:
                go(h_copy(n + 2))
            pass_copy(n).wait_recv()
            over(0, have_w, lambda wc: product(n, 1, wc))
            have_h += 1
            if have_h == tp:
                for s in range(1, INNER):
                    for r in range(outer):
                        send(up_v.at[:, columns((o + r) % outer, inner_of(s))], up_all.at[s, r],
                             us.at[s, r], ur.at[s, r], near(s))

    for copy in local:
        copy.wait()
    for s in range(1, INNER):
        for r in range(outer):
            rdma(up_v.at[:, columns(o, i)], up_all.at[s, r], us.at[s, r], ur.at[s, r], near(s)).wait_recv()

    def gain_of(wc):
        r, j = wc // per, wc % per
        return gain_ref[(o + r) % outer, i, j]

    for s in range(INNER):
        sq = jnp.zeros((tok, 1), jnp.float32)
        al = jnp.zeros((tok, 1), jnp.float32)
        for wc in range(chunks):
            r, j = wc // per, wc % per
            total = stage[wc, t, s].astype(jnp.float32)
            for q in range(1, tp):
                src = (t + q) % tp
                if s % 2 == 0:
                    rs_copy(t, wc, s // 2, src).wait_recv()
                total = total + parts[src, wc, s].astype(jnp.float32)
            merged[s, wc] = total
            along = up_all[s, r, :, j * chunk:(j + 1) * chunk].astype(jnp.float32) * gain_of(wc)
            sq = sq + jnp.sum(total * total, axis=1, keepdims=True)
            al = al + jnp.sum(total * along, axis=1, keepdims=True)
        st[s:s + 1, :] = jnp.swapaxes(jnp.broadcast_to(sq, (tok, 128)), 0, 1)[0:1, :]
        st[INNER + s:INNER + s + 1, :] = jnp.swapaxes(jnp.broadcast_to(al, (tok, 128)), 0, 1)[0:1, :]
    for s in range(1, INNER):
        send(st, st_all.at[s], st_s.at[s], st_r.at[s], near(s))
    for s in range(1, INNER):
        rdma(st, st_all.at[s], st_s.at[s], st_r.at[s], near(s)).wait_recv()

    inverse, proj = [], []
    for s in range(INNER):
        sq, al = st[s:s + 1, :], st[INNER + s:INNER + s + 1, :]
        for q in range(1, INNER):
            k = ((s // 2 + q // 2) % 2) * 2 + (s + q) % 2
            sq = sq + st_all[q, k:k + 1, :]
            al = al + st_all[q, INNER + k:INNER + k + 1, :]
        inv = lax.rsqrt(sq / draft + 1e-05)
        pr = al * inv / draft
        inverse.append(jnp.swapaxes(jnp.broadcast_to(inv, (128, tok)), 0, 1)[:, 0:1])
        proj.append(jnp.swapaxes(jnp.broadcast_to(pr, (128, tok)), 0, 1)[:, 0:1])

    def ag_copy(wc, src, dr):
        side = (dr + 1) // 2
        return rdma(gmt.at[wc, src], gmt.at[wc, src], ag_s.at[wc, side, src],
                    ag_r.at[wc, side, src], {"tp": (t + dr + tp) % tp})

    def ag_own(wc):
        @pl.when(t < tp - 1)
        def _():
            ag_copy(wc, t, 1).start()

        @pl.when(t > 0)
        def _():
            ag_copy(wc, t, -1).start()

    def ag_take(wc, k):
        @pl.when(t - k >= 0)
        def _():
            ag_copy(wc, (t - k + tp) % tp, 1).wait_recv()

            @pl.when(t < tp - 1)
            def _():
                ag_copy(wc, (t - k + tp) % tp, 1).start()

        @pl.when(t + k < tp)
        def _():
            ag_copy(wc, (t + k) % tp, -1).wait_recv()

            @pl.when(t > 0)
            def _():
                ag_copy(wc, (t + k) % tp, -1).start()

    def ag_step(n):
        for k in range(tp - 1, 0, -1):
            m = n + tp - 1 - k
            if 0 <= m < parts_g:
                ag_take(order[m], k)

    def ag_done(wc):
        for k in range(tp):
            @pl.when((t - k >= 0) & (t < tp - 1))
            def _():
                ag_copy(wc, (t - k + tp) % tp, 1).wait_send()

            @pl.when((t + k < tp) & (t > 0))
            def _():
                ag_copy(wc, (t + k) % tp, -1).wait_send()

    order = list(range(per_g, parts_g)) + list(range(per_g))
    for g in order:
        r, j, wc = g // per_g, g % per_g, g // split
        here = slice(j * part, (j + 1) * part)
        sub = slice((g % split) * part, (g % split + 1) * part)
        gain = gain_of(wc)[:, sub]
        own = jnp.zeros((1, part), jnp.float32)
        for s in range(INNER):
            scaled = merged[s, wc, :, sub] * inverse[s]
            incoming = up_all[s, r, :, here].astype(jnp.float32)
            norm_buf[s, r, :, here] = (scaled * gain).astype(jnp.bfloat16)
            own = own + jnp.sum(incoming * scaled, axis=0, keepdims=True)
            grad = inverse[s] * (incoming * gain - scaled * proj[s])
            gmt[g, t, :, s * tok:(s + 1) * tok] = jnp.swapaxes(grad, 0, 1).astype(jnp.bfloat16)
        gg[wc:wc + 1, sub] = own
        if g in order[:tp - 1]:
            ag_own(g)

    for s in range(1, INNER):
        for r in range(outer):
            send(norm_buf.at[s, r], normed_ref.at[:, columns((o + r) % outer, i)],
                 ns.at[s, r], nr.at[s, r], near(s))
    keep = []
    for r in range(outer):
        copy = pltpu.make_async_copy(norm_buf.at[0, r], normed_ref.at[:, columns((o + r) % outer, i)],
                                     local_sem.at[2 + r])
        copy.start()
        keep.append(copy)
    for q in range(1, tp):
        send(gg, gg_tp.at[tp - q], g1s.at[q], g1r.at[tp - q], {"tp": (t + q) % tp})

    def gain_step(n):
        if n == 0:
            total = gg[...]
            for q in range(1, tp):
                rdma(gg, gg_tp.at[q], g1s.at[q], g1r.at[q], {"tp": (t + q) % tp}).wait_recv()
                total = total + gg_tp[q]
            gg_out[0] = total
            for r in range(1, outer):
                send(gg_out.at[0], gg_out.at[outer - r], g2s.at[r], g2r.at[outer - r], far(r))
        if n == 1:
            for r in range(1, outer):
                rdma(gg_out.at[0], gg_out.at[r], g2s.at[r], g2r.at[r], far(r)).wait_recv()
            for wc in range(chunks):
                total = gg_out[0, wc:wc + 1, :]
                for r in range(1, outer):
                    k = (wc - r * per) % chunks
                    total = total + gg_out[r, k:k + 1, :]
                gg_in[0, wc:wc + 1, :] = total
            for s in range(1, INNER):
                send(gg_in.at[0], gg_in.at[s], g3s.at[s], g3r.at[s], near(s))
        if n == 2:
            for s in range(1, INNER):
                rdma(gg_in.at[0], gg_in.at[s], g3s.at[s], g3r.at[s], near(s)).wait_recv()
            for s in range(INNER):
                for wc in range(chunks):
                    gg_ref[(o + wc // per) % outer, inner_of(s), wc % per] = gg_in[s, wc:wc + 1, :]

    tile = min(512, slab)

    def g_copy(k, l, r):
        return rdma(gstage.at[k, l], grecv.at[outer - r - 1, l, k % per_g], gs.at[k, l],
                    gr.at[outer - r - 1, l, k % per_g], far(r))

    for n in range(2 - tp, 0):
        ag_step(n)
    for n, g in enumerate(order):
        ag_step(n)
        if n + tp - 1 < parts_g:
            ag_own(order[n + tp - 1])
        for l in range(layers):
            def step(k, carry):
                cols = pl.ds(pl.multiple_of(k * tile, 128), tile)
                acc = jnp.zeros((part, tile), jnp.float32)
                for z in range(tp):
                    right = h_all[l, z, :, :, cols].reshape(INNER * tok, tile)
                    acc = acc + jnp.dot(gmt[g, z], right, preferred_element_type=jnp.float32)
                if g >= per_g:
                    gstage[g - per_g, l, :, cols] = acc.astype(jnp.bfloat16)
                else:
                    gown[l, g, :, cols] = acc.astype(jnp.bfloat16)
                return carry
            lax.fori_loop(0, slab // tile, step, 0)
            if g >= per_g:
                go(g_copy(g - per_g, l, g // per_g))
            else:
                copy = pltpu.make_async_copy(gown.at[l, g], gown_ref.at[l, g], go_s.at[l, g])
                copy.start()
                keep.append(copy)
        if n % 2 == 1:
            gain_step(n // 2)
    for r in range(1, outer):
        for j in range(per_g):
            for l in range(layers):
                rdma(gstage.at[0, l], grecv.at[r - 1, l, j], gs.at[j, l], gr.at[r - 1, l, j], far(r)).wait_recv()

    for s in range(1, INNER):
        for r in range(outer):
            rdma(norm_buf.at[s, r], normed_ref.at[:, columns((o + r) % outer, inner_of(s))],
                 ns.at[s, r], nr.at[s, r], near(s)).wait_recv()
    for copy in keep:
        copy.wait()
    for copy in started:
        copy.wait_send()
    for g in range(parts_g):
        ag_done(g)
    for wc in range(chunks):
        for a in range(INNER // 2):
            for q in range(1, tp):
                rs_copy((t + q) % tp, wc, a, t).wait_send()


def body(dp, tp, hidden_states, fc_weight, norm_gain, upstream, lengths):
    tok_group, layers, slab = hidden_states.shape
    rows = fc_weight.shape[0]
    tok, draft = upstream.shape
    depth = layers * slab
    outer = dp // INNER
    chunk = min(256, rows)
    per = rows // chunk
    chunks = outer * per
    bf, f32 = jnp.bfloat16, jnp.float32
    part = min(128, chunk)
    parts_g, per_g = rows * outer // part, rows // part
    dma = pltpu.SemaphoreType.DMA
    hbm = pl.BlockSpec(memory_space=pl.ANY)
    vmem = pl.BlockSpec(memory_space=pltpu.VMEM)
    flops = 4 * tok_group * draft * depth
    normed, own, others, gg = pl.pallas_call(
        functools.partial(kernel, dp, tp),
        out_shape=(jax.ShapeDtypeStruct((tok, draft), bf),
                   jax.ShapeDtypeStruct((layers, per_g, part, slab), bf),
                   jax.ShapeDtypeStruct((max(1, outer - 1), layers, per_g, part, slab), bf),
                   jax.ShapeDtypeStruct((outer, INNER, per, 1, chunk), f32)),
        in_specs=[hbm, hbm, hbm, vmem, pl.BlockSpec(memory_space=pltpu.SMEM)],
        out_specs=(hbm, hbm, hbm, vmem),
        scratch_shapes=[
            pltpu.VMEM((layers, tp, INNER, tok, slab), bf),
            pltpu.VMEM((layers, chunks, chunk, slab), bf),
            pltpu.VMEM((chunks, tp, INNER, tok, chunk), bf),
            pltpu.VMEM((tp, chunks, INNER, tok, chunk), bf),
            pltpu.VMEM((INNER, chunks, tok, chunk), f32),
            pltpu.VMEM((INNER, outer, tok, rows), bf),
            pltpu.VMEM((INNER, outer, tok, rows), bf),
            pltpu.VMEM((parts_g, tp, part, INNER * tok), bf),
            pltpu.VMEM((max(1, parts_g - per_g), layers, part, slab), bf),
            pltpu.VMEM((layers, per_g, part, slab), bf),
            pltpu.VMEM((tok, draft), bf),
            pltpu.VMEM((2 * INNER, tok), f32),
            pltpu.VMEM((INNER, 2 * INNER, tok), f32),
            pltpu.VMEM((chunks, chunk), f32),
            pltpu.VMEM((tp, chunks, chunk), f32),
            pltpu.VMEM((outer, chunks, chunk), f32),
            pltpu.VMEM((INNER, chunks, chunk), f32),
            dma((2 + outer,)),
            dma((3, tp)), dma((INNER, tp)),
            dma((chunks * layers,)), dma((chunks * layers,)),
            dma((INNER, outer)), dma((INNER, outer)),
            dma((tp, chunks, INNER // 2)), dma((tp, chunks, INNER // 2)),
            dma((INNER,)), dma((INNER,)),
            dma((parts_g, 2, tp)), dma((parts_g, 2, tp)),
            dma((INNER, outer)), dma((INNER, outer)),
            dma((max(1, parts_g - per_g), layers)), dma((max(1, outer - 1), layers, per_g)),
            dma((layers, per_g)),
            dma((tp,)), dma((tp,)),
            dma((outer,)), dma((outer,)),
            dma((INNER,)), dma((INNER,)),
        ],
        compiler_params=pltpu.CompilerParams(collective_id=0, has_side_effects=True,
                                             vmem_limit_bytes=62 * 2**20),
        cost_estimate=pl.CostEstimate(flops=flops, bytes_accessed=8 * tok_group * depth,
                                      transcendentals=0),
    )(hidden_states.transpose(1, 0, 2).reshape(layers, tp, tok, slab),
      fc_weight.transpose(1, 0, 2).reshape(layers, per, chunk, slab), upstream,
      norm_gain.reshape(outer, INNER, per, 1, chunk), lengths)
    gw = own.astype(f32)
    for r in range(outer - 1):
        gw = gw + others[r].astype(f32)
    return normed, gw.reshape(layers, rows, slab).transpose(1, 0, 2), gg.reshape(draft)


def solution(mesh):
    return jax.shard_map(
        functools.partial(body, mesh.shape["dp"], mesh.shape["tp"]),
        mesh=mesh,
        in_specs=(
            P("dp", None, "tp"),
            P("dp", None, "tp"),
            P(),
            P(("dp", "tp"), None),
            P(("dp", "tp")),
        ),
        out_specs=(P(("dp", "tp"), None), P("dp", None, "tp"), P()),
        check_vma=False,
    )
```
